128 devices in a mesh: dp: 32 (over y, z, core), mp: 4 (over x).
Axes of the slice: x: 4, y: 4, z: 4, core: 2. Of those that a mesh axis runs over, the one named last changes fastest.
Arguments:
- hidden: bfloat16 [8192, 8192], P('dp', 'mp'), may hold values from -6 to 6
- base_query_rows: bfloat16 [8192, 8192], P('dp', 'mp'), may hold values from -6 to 6
- key_value_base: bfloat16 [8192, 2, 1024], P('dp', None, 'mp'), may hold values from -6 to 6
- key_value_pool: bfloat16 [8192, 2, 16, 1024], P('dp', None, None, 'mp'), may hold values from -28 to 28
- request_page_table: int32 [8192, 16], P('dp'), may hold values from 0 to 319
- context_length: int32 [8192], P('dp'), may hold values from 1 to 256
- handover_pages: int32 [1024, 2], P('dp'), may hold values from 0 to 255
- request_adapter: int32 [8192], P('dp'), may hold values from 0 to 511, as said below
- adapter_position: int32 [512], replicated, may hold values from 0 to 511, as said below
- adapter_down_weight: bfloat16 [512, 3, 64, 8192], P('dp', None, None, 'mp'), may hold values from -0.0625 to 0.0625
- query_up_weight: bfloat16 [512, 64, 8192], P('dp', None, 'mp'), may hold values from -0.75 to 0.75
- key_value_up: bfloat16 [512, 2, 64, 1024], P('dp', None, None, 'mp'), may hold values from -0.75 to 0.75
Outputs:
- attended: bfloat16 [8192, 8192], P('dp', 'mp')
The draws below stay inside these ranges and needn't reach their ends.
Inputs may be any that keep to these rules, and one draw needn't show every extreme that they name: `request_adapter`: among the requests of one index of dp, at most 16 use adapters whose slots lie with one owner, and in every such block some owner has exactly 16 of them. `adapter_position`: each adapter has a slot of its own.
All inputs are finite; a program needn't handle non-finite values.
Results may differ from the reference program's by a relative error of at most 0.009.
Values may be sent and summed in bfloat16 or wider, within the bound.
A program may use at most 128 MiB of HBM per device.

```python
import jax
import jax.numpy as jnp
from jax import lax

MODEL_WIDTH = 8192
HQ = 64
KEY_VALUE_HEADS = 8
HEAD_SIZE = 128
ADAPTER_RANK = 64
ADP = 16
ADAPTER_TOTAL = 512
ROWS_DEV = 256
REQUEST_TOTAL = 8192
CAP = 16
PAGE_TOKENS = 16
PPR = 16
POOL_PAGES = 256
MCAP = 2
EXT = 320
N_DP = 32


def routing(key):
    key_perm, key_blocks = jax.random.split(key, 2)
    slots = jax.random.permutation(key_perm, ADAPTER_TOTAL).astype(jnp.int32)
    adapter_at = jnp.argsort(slots).astype(jnp.int32)

    def one_block(block_key):
        key_one, key_two, key_three, key_four = jax.random.split(block_key, 4)
        cells = jnp.arange(N_DP * CAP, dtype=jnp.int32)
        scores = jax.random.permutation(key_one, N_DP * CAP).astype(jnp.int32)
        forced = jax.random.randint(key_two, (), 0, N_DP, dtype=jnp.int32)
        scores = jnp.where(cells // CAP == forced, scores - N_DP * CAP, scores)
        chosen = (jnp.argsort(scores)[:ROWS_DEV] // CAP).astype(jnp.int32)
        chosen = jax.random.permutation(key_three, chosen)
        within = jax.random.randint(key_four, (ROWS_DEV,), 0, ADP, dtype=jnp.int32)
        return chosen * ADP + within
    owned = jax.vmap(one_block)(jax.random.split(key_blocks, N_DP)).reshape(-1)
    return (slots, adapter_at[owned].astype(jnp.int32))


def draw_request_adapter(key, part):
    return routing(key)[1]


def draw_adapter_position(key, part):
    return routing(key)[0]


def draw_key_value_pool(key, part):
    key = jax.random.fold_in(key, 7)
    key_one = jax.random.fold_in(key, 0)
    array_shape = (N_DP * POOL_PAGES, 2, PAGE_TOKENS, KEY_VALUE_HEADS * HEAD_SIZE)
    values = jnp.clip(jax.random.normal(key_one, array_shape, jnp.float32), -6.0, 6.0)
    return values.astype(jnp.bfloat16)


def set_ends(array, own_key, least, top_value):
    spot = [jax.random.randint(jax.random.fold_in(own_key, axis), (), 0, length) for axis, length in enumerate(array.shape)]
    main_axis = array.shape.index(max(array.shape))
    next_to = spot[:main_axis] + [(spot[main_axis] + 1) % array.shape[main_axis]] + spot[main_axis + 1:]
    return array.at[tuple(spot)].set(least).at[tuple(next_to)].set(top_value)


def steps_of(own_key, dims, shards, least, high):
    factor_of = 1.0
    for position, parts in shards:
        steps = jax.random.uniform(jax.random.fold_in(jax.random.fold_in(own_key, 6), position), (parts,), jnp.float32, least / len(shards), high / len(shards))
        factor_of = factor_of * jnp.repeat(jnp.exp(steps), dims[position] // parts).reshape((-1,) + (1,) * (len(dims) - 1 - position))
    return factor_of


def noise(stream_key, shape, spread, most, shards=(), kind=jnp.bfloat16):
    loudness = steps_of(stream_key, shape, shards, -0.22, 0.18) if shards else 1.0
    drawn = jax.random.normal(stream_key, shape, jnp.float32) * spread * loudness
    return jnp.minimum(jnp.maximum(drawn, -most), most).astype(kind)


def setup_inputs(seed: int = 0) -> dict:
    streams_of = jax.random.split(jax.random.key(seed), 13)
    return {
        "hidden": noise(streams_of[0], (REQUEST_TOTAL, MODEL_WIDTH), 1.0, 6.0, ((0, 32), (1, 4))),
        "base_query_rows": noise(streams_of[1], (REQUEST_TOTAL, HQ * HEAD_SIZE), 1.0, 6.0, ((0, 32), (1, 4))),
        "key_value_base": noise(streams_of[2], (REQUEST_TOTAL, 2, KEY_VALUE_HEADS * HEAD_SIZE), 1.0, 6.0, ((0, 32), (2, 4))),
        "key_value_pool": draw_key_value_pool(jax.random.fold_in(streams_of[12], 71), 0),
        "request_page_table": set_ends(jax.random.randint(streams_of[4], (REQUEST_TOTAL, PPR), 0, EXT), jax.random.fold_in(streams_of[4], 1), 0, EXT - 1).astype(jnp.int32),
        "context_length": set_ends(jax.random.randint(streams_of[5], (REQUEST_TOTAL,), 1, PPR * PAGE_TOKENS + 1), jax.random.fold_in(streams_of[5], 1), 1, PPR * PAGE_TOKENS).astype(jnp.int32),
        "handover_pages": set_ends(jax.random.randint(streams_of[6], (N_DP * N_DP, MCAP), 0, POOL_PAGES), jax.random.fold_in(streams_of[6], 1), 0, POOL_PAGES - 1).astype(jnp.int32),
        "request_adapter": draw_request_adapter(jax.random.fold_in(streams_of[12], 71), 0),
        "adapter_position": draw_adapter_position(jax.random.fold_in(streams_of[12], 71), 0),
        "adapter_down_weight": noise(streams_of[9], (ADAPTER_TOTAL, 3, ADAPTER_RANK, MODEL_WIDTH), MODEL_WIDTH ** -0.5, 0.0625, ((0, 32), (3, 4))),
        "query_up_weight": noise(streams_of[10], (ADAPTER_TOTAL, ADAPTER_RANK, HQ * HEAD_SIZE), ADAPTER_RANK ** -0.5, 0.75, ((0, 32), (2, 4))),
        "key_value_up": noise(streams_of[11], (ADAPTER_TOTAL, 2, ADAPTER_RANK, KEY_VALUE_HEADS * HEAD_SIZE), ADAPTER_RANK ** -0.5, 0.75, ((0, 32), (3, 4))),
    }


adapter_scale = 0.5


def rank_block_product(call_arguments, adapter_down_weight, query_up_weight, key_value_up):
    rows_blk, slot_block = call_arguments
    down_weight = adapter_down_weight[slot_block].astype(jnp.float32)
    low = jnp.einsum("rd,rjcd->rjc", rows_blk.astype(jnp.float32), down_weight)
    low = lax.optimization_barrier(low.astype(jnp.bfloat16)).astype(jnp.float32)
    up_query = query_up_weight[slot_block].astype(jnp.float32)
    up_kv = key_value_up[slot_block].astype(jnp.float32)
    query_delta_rows = jnp.einsum("rc,rce->re", low[:, 0], up_query)
    key_delta_rows = jnp.einsum("rc,rce->re", low[:, 1], up_kv[:, 0])
    value_delta_rows = jnp.einsum("rc,rce->re", low[:, 2], up_kv[:, 1])
    update_delta = adapter_scale * jnp.concatenate([query_delta_rows, key_delta_rows, value_delta_rows], axis=1)
    return update_delta.astype(jnp.bfloat16)


def attend(query, key_new, value_new, pages, lengths):
    count = query.shape[0]
    heads_kv = key_new.shape[1] // HEAD_SIZE
    groups = query.shape[1] // (heads_kv * HEAD_SIZE)
    keys = pages[:, :, 0].reshape(count, -1, heads_kv, HEAD_SIZE).astype(jnp.float32)
    values = pages[:, :, 1].reshape(count, -1, heads_kv, HEAD_SIZE).astype(jnp.float32)
    heads = query.reshape(count, heads_kv, groups, HEAD_SIZE).astype(jnp.float32)
    factor = HEAD_SIZE ** -0.5
    scores = jnp.einsum("bhgd,bthd->bhgt", heads, keys) * factor
    own = jnp.einsum("bhgd,bhd->bhg", heads, key_new.reshape(count, heads_kv, HEAD_SIZE).astype(jnp.float32)) * factor
    valid = jnp.arange(keys.shape[1], dtype=jnp.int32)[None, :] < lengths[:, None]
    scores = jnp.where(valid[:, None, None, :], scores, -jnp.inf)
    top = jnp.maximum(jnp.max(scores, axis=-1), own)
    probs = jnp.exp(scores - top[..., None])
    own_p = jnp.exp(own - top)
    total = jnp.sum(probs, axis=-1) + own_p
    weights = lax.optimization_barrier((probs / total[..., None]).astype(jnp.bfloat16)).astype(jnp.float32)
    own_w = lax.optimization_barrier((own_p / total).astype(jnp.bfloat16)).astype(jnp.float32)
    out = jnp.einsum("bhgt,bthd->bhgd", weights, values)
    out = out + own_w[..., None] * value_new.reshape(count, heads_kv, 1, HEAD_SIZE).astype(jnp.float32)
    return out.reshape(count, -1).astype(jnp.bfloat16)


def reference(hidden, base_query_rows, key_value_base, key_value_pool, request_page_table, context_length, handover_pages, request_adapter, adapter_position, adapter_down_weight, query_up_weight, key_value_up):
    query_width = HQ * HEAD_SIZE
    key_value_width = KEY_VALUE_HEADS * HEAD_SIZE
    slot_rows = adapter_position[request_adapter].astype(jnp.int32)
    blocks = REQUEST_TOTAL // 16
    update_delta = lax.map(lambda adapter_array: rank_block_product(adapter_array, adapter_down_weight, query_up_weight, key_value_up),
                    (hidden.reshape(blocks, 16, MODEL_WIDTH), slot_rows.reshape(blocks, 16)))
    update_delta = update_delta.reshape(REQUEST_TOTAL, query_width + 2 * key_value_width)
    query_delta_rows = lax.optimization_barrier(update_delta[:, :query_width]).astype(jnp.float32)
    delta_kv = lax.optimization_barrier(update_delta[:, query_width:]).astype(jnp.float32).reshape(REQUEST_TOTAL, 2, key_value_width)
    query = (base_query_rows.astype(jnp.float32) + query_delta_rows).astype(jnp.bfloat16)
    fresh = (key_value_base.astype(jnp.float32) + delta_kv).astype(jnp.bfloat16)
    pool = key_value_pool.reshape(N_DP, POOL_PAGES, 2, PAGE_TOKENS, key_value_width)
    lists = handover_pages.reshape(N_DP, N_DP, MCAP)
    sources = jnp.arange(N_DP, dtype=jnp.int32)[:, None]

    def per_device(index):
        incoming = pool[sources, lists[:, index]].reshape(N_DP * MCAP, 2, PAGE_TOKENS, key_value_width)
        extended = jnp.concatenate([pool[index], incoming], axis=0)
        start = (index * ROWS_DEV).astype(jnp.int32)
        dev_query = lax.dynamic_slice_in_dim(query, start, ROWS_DEV).reshape(ROWS_DEV // 16, 16, query_width)
        dev_fresh = lax.dynamic_slice_in_dim(fresh, start, ROWS_DEV).reshape(ROWS_DEV // 16, 16, 2, key_value_width)
        dev_table = lax.dynamic_slice_in_dim(request_page_table, start, ROWS_DEV).reshape(ROWS_DEV // 16, 16, PPR)
        dev_len = lax.dynamic_slice_in_dim(context_length, start, ROWS_DEV).reshape(ROWS_DEV // 16, 16)

        def one_block(call_arguments):
            q_blk, f_blk, t_blk, l_blk = call_arguments
            return attend(q_blk, f_blk[:, 0], f_blk[:, 1], extended[t_blk], l_blk)

        return lax.map(one_block, (dev_query, dev_fresh, dev_table, dev_len)).reshape(ROWS_DEV, query_width)

    out = lax.map(per_device, jnp.arange(N_DP, dtype=jnp.int32))
    return out.reshape(REQUEST_TOTAL, query_width)
```

```python
import jax
import jax.numpy as jnp
from jax import lax
from jax.experimental import pallas as pl
from jax.experimental.pallas import tpu as pltpu
from jax.sharding import PartitionSpec as P

HEAD_SIZE = 128
PAGE_TOKENS = 16
MCAP = 2


adapter_scale = 0.5


def lookup(ids, table):
    hits = ids[:, None] == jnp.arange(table.shape[0], dtype=jnp.int32)[None, :]
    return jnp.sum(jnp.where(hits, table[None, :], 0), axis=1)


def route_rows(slot_rows, owners, owner_grouping, capacity):
    owner = slot_rows // owner_grouping
    marks = (owner[:, None] == jnp.arange(owners, dtype=jnp.int32)[None, :]).astype(jnp.int32)
    before = jnp.cumsum(marks, axis=0) - marks
    position = jnp.sum(before * marks, axis=1)
    return owner * capacity + position


def build_update_delta(
    flattened_rows,
    local_indices,
    adapter_down_weight,
    query_up_weight,
    key_value_up,
    reduce_rank_partial,
):
    slots_in = flattened_rows.shape[0]
    owner_grouping = adapter_down_weight.shape[0]
    adapter_rank_size = adapter_down_weight.shape[2]
    width_portion = flattened_rows.shape[1]
    query_part = query_up_weight.shape[2]
    kv_part = key_value_up.shape[3]
    flattened_down = adapter_down_weight.reshape(
        owner_grouping * 3 * adapter_rank_size, width_portion
    )
    projected = lax.dot_general(
        flattened_rows, flattened_down, (((1,), (1,)), ((), ())), preferred_element_type=jnp.float32
    )
    projected = projected.reshape(slots_in, owner_grouping, 3 * adapter_rank_size)
    picked = (
        local_indices[:, None] == jnp.arange(owner_grouping, dtype=jnp.int32)[None, :]
    ).astype(jnp.float32)
    partial_low = jnp.einsum("mk,mkc->mc", picked, projected)
    low = reduce_rank_partial(partial_low).astype(jnp.bfloat16)
    spread = (picked.astype(jnp.bfloat16)[:, :, None] * low[:, None, :]).reshape(
        slots_in, owner_grouping, 3, adapter_rank_size
    )
    query_delta_rows = jnp.dot(
        spread[:, :, 0, :].reshape(slots_in, owner_grouping * adapter_rank_size),
        query_up_weight.reshape(owner_grouping * adapter_rank_size, query_part),
        preferred_element_type=jnp.float32,
    )
    key_delta_rows = jnp.dot(
        spread[:, :, 1, :].reshape(slots_in, owner_grouping * adapter_rank_size),
        key_value_up[:, 0].reshape(owner_grouping * adapter_rank_size, kv_part),
        preferred_element_type=jnp.float32,
    )
    value_delta_rows = jnp.dot(
        spread[:, :, 2, :].reshape(slots_in, owner_grouping * adapter_rank_size),
        key_value_up[:, 1].reshape(owner_grouping * adapter_rank_size, kv_part),
        preferred_element_type=jnp.float32,
    )
    return (
        adapter_scale
        * jnp.concatenate([query_delta_rows, key_delta_rows, value_delta_rows], axis=1)
    ).astype(jnp.bfloat16)


def attend_kernel(table, lens, target_ref, back_ref, baseq_ref, basekv_ref, pool_ref, mig_ref, out_ref, ext, fresh, wide):
    rows, heads = wide.shape[0], wide.shape[1]
    pages, per = pool_ref.shape[0], table.shape[1]
    D = 128; T = 16; group = 16
    half = heads // 2
    ext[:pages] = pool_ref[...]
    ext[pages:] = mig_ref[...]
    slots = back_ref.shape[0]
    pick = (lax.broadcasted_iota(jnp.int32, (rows, slots), 1) == target_ref[...]).astype(jnp.bfloat16)
    for h in range(heads):
        part = jnp.dot(pick, back_ref[:, h*D:(h+1)*D], preferred_element_type=jnp.float32)
        wide[:, h, :] = (baseq_ref[:, h*D:(h+1)*D].astype(jnp.float32) + part).astype(jnp.bfloat16).astype(jnp.float32)
    part = jnp.dot(pick, back_ref[:, heads*D:], preferred_element_type=jnp.float32)
    fresh[...] = (basekv_ref[...].astype(jnp.float32) + part).astype(jnp.bfloat16).astype(jnp.float32)
    tok = lax.broadcasted_iota(jnp.int32, (heads, per*T), 1)
    first = lax.broadcasted_iota(jnp.int32, (heads, D), 0) < half
    scale = D ** -0.5
    def gather(r, which):
        return jnp.concatenate([ext[table[r, p], which] for p in range(per)], axis=0)
    def two(r, at):
        row = fresh[pl.ds(r, 1), at:at + 2*D]
        return jnp.concatenate([jnp.broadcast_to(row[:, :D], (half, D)), jnp.broadcast_to(row[:, D:], (half, D))], axis=0)
    def score(r):
        q = wide[r]
        zero = jnp.zeros_like(q)
        both = jnp.concatenate([jnp.where(first, q, zero), jnp.where(first, zero, q)], axis=1).astype(jnp.bfloat16)
        return lax.dot_general(both, gather(r, 0), (((1,), (1,)), ((), ())), preferred_element_type=jnp.float32)
    def soft(r, s):
        s = jnp.where(tok < lens[0, r], s * scale, -jnp.inf)
        own = jnp.sum(wide[r] * two(r, 0), axis=1, keepdims=True) * scale
        top = jnp.maximum(jnp.max(s, axis=1, keepdims=True), own)
        p = jnp.exp(s - top)
        po = jnp.exp(own - top)
        inv = 1.0 / (jnp.sum(p, axis=1, keepdims=True) + po)
        return (p * inv).astype(jnp.bfloat16), (po * inv).astype(jnp.bfloat16).astype(jnp.float32) * two(r, 2*D)
    def weigh(r, p, ov):
        o = jnp.dot(p, gather(r, 1), preferred_element_type=jnp.float32)
        wide[r] = jnp.where(first, o[:, :D], o[:, D:]) + ov
    def body(i, c):
        ss = [score(i*group+j) for j in range(group)]
        pp = [soft(i*group+j, ss[j]) for j in range(group)]
        for j in range(group): weigh(i*group+j, *pp[j])
        return c
    lax.fori_loop(0, rows // group, body, 0)
    for h in range(heads):
        out_ref[:, h*D:(h+1)*D] = wide[:, h, :].astype(jnp.bfloat16)

def attend(table, lens, target, back, baseq, basekv, pool, mig):
    rows, width = baseq.shape
    vm = pl.BlockSpec(memory_space=pltpu.VMEM)
    sm = pl.BlockSpec(memory_space=pltpu.SMEM)
    return pl.pallas_call(attend_kernel,
        out_shape=jax.ShapeDtypeStruct((rows, width), jnp.bfloat16),
        in_specs=[sm, sm] + [vm]*6, out_specs=vm,
        scratch_shapes=[pltpu.VMEM((pool.shape[0]+mig.shape[0],)+pool.shape[1:], jnp.bfloat16), pltpu.VMEM(basekv.shape, jnp.float32), pltpu.VMEM((rows, width//128, 128), jnp.float32)],
        compiler_params=pltpu.CompilerParams(vmem_limit_bytes=56*1024*1024),
    )(table, lens, target, back, baseq, basekv, pool, mig)

def shards(
    hidden,
    base_query_rows,
    key_value_base,
    key_value_pool,
    request_page_table,
    context_length,
    handover_pages,
    request_adapter,
    adapter_position,
    adapter_down_weight,
    query_up_weight,
    key_value_up,
):
    owners = lax.axis_size("dp")
    me = lax.axis_index("dp")
    rows = hidden.shape[0]
    capacity = 2 * rows // owners
    owner_grouping = adapter_down_weight.shape[0]
    width_portion = hidden.shape[1]
    query_part = base_query_rows.shape[1]
    kv_part = key_value_base.shape[2]
    total_slots = owners * capacity
    slot_rows = lookup(request_adapter, adapter_position)
    target = route_rows(slot_rows, owners, owner_grouping, capacity)
    placed = target[None, :] == jnp.arange(total_slots, dtype=jnp.int32)[:, None]
    placement = placed.astype(jnp.bfloat16)
    tags = jnp.broadcast_to(
        (slot_rows % owner_grouping).astype(jnp.bfloat16)[:, None], (rows, HEAD_SIZE)
    )
    send_rows = jnp.dot(
        placement, jnp.concatenate([hidden, tags], axis=1), preferred_element_type=jnp.float32
    ).astype(jnp.bfloat16)
    send_rows = send_rows.reshape(owners, capacity, width_portion + HEAD_SIZE)
    leaving_pages = key_value_pool[handover_pages]
    arrived = lax.all_to_all(send_rows, "dp", split_axis=0, concat_axis=0, tiled=True)
    migrated = lax.all_to_all(leaving_pages, "dp", split_axis=0, concat_axis=0, tiled=True)
    arrived = arrived.reshape(total_slots, width_portion + HEAD_SIZE)
    arriving_local = arrived[:, width_portion].astype(jnp.int32)
    update_delta = build_update_delta(
        arrived[:, :width_portion],
        arriving_local,
        adapter_down_weight,
        query_up_weight,
        key_value_up,
        lambda partial_low: lax.psum(partial_low, "mp"),
    )
    returned = lax.all_to_all(
        update_delta.reshape(owners, capacity, query_part + 2 * kv_part),
        "dp",
        split_axis=0,
        concat_axis=0,
        tiled=True,
    )
    returned_flat = returned.reshape(total_slots, query_part + 2 * kv_part)
    return attend(
        request_page_table,
        context_length.reshape(1, rows),
        target.reshape(rows, 1),
        returned_flat,
        base_query_rows,
        key_value_base.reshape(rows, 2 * kv_part),
        key_value_pool,
        migrated.reshape(owners * MCAP, 2, PAGE_TOKENS, kv_part),
    )


def solution(mesh):
    return jax.shard_map(
        shards,
        mesh=mesh,
        in_specs=(
            P("dp", "mp"),
            P("dp", "mp"),
            P("dp", None, "mp"),
            P("dp", None, None, "mp"),
            P("dp", None),
            P("dp"),
            P("dp", None),
            P("dp"),
            P(),
            P("dp", None, None, "mp"),
            P("dp", None, "mp"),
            P("dp", None, None, "mp"),
        ),
        out_specs=P("dp", "mp"),
        check_vma=False,
    )
```

```python
import jax
import jax.numpy as jnp
from jax import lax
from jax.experimental import pallas as pl
from jax.experimental.pallas import tpu as pltpu
from jax.sharding import PartitionSpec as P

HEAD_SIZE = 128
PAGE_TOKENS = 16
MCAP = 2
CAPACITY = 16
GROUP = 16
MESH = pl.DeviceIdType.MESH

adapter_scale = 0.5


def torus_offsets():
    near = [(1, 0), (0, 1), (3, 0), (0, 3)]
    diagonal = [(1, 1), (3, 3), (1, 3), (3, 1)]
    bent = [(2, 1), (1, 2), (2, 3), (3, 2)]
    straight = [(2, 0), (0, 2)]
    order = [(0, 0, 0), (0, 0, 1)]
    for chips in (near, diagonal, bent, straight, [(2, 2)]):
        for core in (0, 1):
            order += [(y, z, core) for y, z in chips]
    return order


OFFSETS = torus_offsets()
SENDS = [[(0, 0)], [(0, 1)], [(0, 2), (1, 0), (1, 1)], [(0, 3), (1, 2), (1, 3)]]


def fused(
    ids_hbm,
    place_hbm,
    table_hbm,
    lens_hbm,
    handover_hbm,
    hidden_hbm,
    base_query_hbm,
    base_kv_hbm,
    pool_hbm,
    down_hbm,
    query_up_hbm,
    kv_up_hbm,
    out_hbm,
    ids_row,
    place_row,
    table,
    lens,
    handover,
    out_ref,
    hidden,
    base_query,
    base_kv,
    base_new,
    down,
    query_up,
    kv_up,
    sent,
    arrived,
    leaving,
    landing,
    ext,
    low,
    part,
    gathered,
    delta,
    back,
    wide,
    fresh,
    load_sem,
    row_send,
    row_recv,
    page_send,
    page_recv,
    sum_send,
    sum_recv,
    back_send,
    back_recv,
):
    rows, width = hidden.shape
    slots = arrived.shape[0]
    owners = slots // CAPACITY
    adapters, _, rank, _ = down.shape
    pages = pool_hbm.shape[0]
    page_count = table.shape[0]
    D = HEAD_SIZE
    kv_heads = base_kv.shape[2] // D
    per_head = base_query.shape[1] // (kv_heads * D)
    chunk = (per_head + 2) * D
    blocks, packed = part.shape[0], part.shape[1]
    block = slots // blocks
    half_block = block // 2
    group_devices = block // CAPACITY

    loads = [
        pltpu.make_async_copy(hidden_hbm, hidden, load_sem.at[0]),
        pltpu.make_async_copy(pool_hbm, ext.at[pl.ds(0, pages)], load_sem.at[1]),
        pltpu.make_async_copy(down_hbm, down, load_sem.at[2]),
        pltpu.make_async_copy(query_up_hbm, query_up, load_sem.at[3]),
        pltpu.make_async_copy(kv_up_hbm, kv_up, load_sem.at[4]),
        pltpu.make_async_copy(base_query_hbm, base_query, load_sem.at[5]),
        pltpu.make_async_copy(base_kv_hbm, base_kv, load_sem.at[6]),
        pltpu.make_async_copy(ids_hbm, ids_row, load_sem.at[7]),
        pltpu.make_async_copy(place_hbm, place_row, load_sem.at[8]),
        pltpu.make_async_copy(handover_hbm, handover, load_sem.at[9]),
        pltpu.make_async_copy(table_hbm, table, load_sem.at[10]),
        pltpu.make_async_copy(lens_hbm, lens, load_sem.at[11]),
    ]
    for k in (7, 8, 0, 9, 1, 10, 11):
        loads[k].start()

    me = lax.axis_index("dp")
    mine = lax.axis_index("mp")
    y, z, core = me // 8, (me // 2) % 4, me % 2

    def ahead(o):
        return ((y + o[0]) % 4) * 8 + ((z + o[1]) % 4) * 2 + (core + o[2]) % 2

    def behind(o):
        return ((y + 4 - o[0]) % 4) * 8 + ((z + 4 - o[1]) % 4) * 2 + (core + o[2]) % 2

    def iota(shape, axis):
        return lax.broadcasted_iota(jnp.int32, shape, axis)

    barrier = pltpu.get_barrier_semaphore()
    for o in OFFSETS[1:]:
        pl.semaphore_signal(barrier, inc=1, device_id={"dp": ahead(o)}, device_id_type=MESH)
    for step in range(1, 4):
        pl.semaphore_signal(
            barrier, inc=1, device_id={"mp": (mine + step) % 4}, device_id_type=MESH
        )

    loads[7].wait()
    loads[8].wait()
    total = place_row.shape[1]
    first_index, second_index = iota((rows, rows), 0), iota((rows, rows), 1)
    diagonal = first_index == second_index
    ids_col = jnp.sum(jnp.where(diagonal, ids_row[...], 0), axis=1, keepdims=True)
    slot_col = jnp.sum(
        jnp.where(iota((rows, total), 1) == ids_col, place_row[...], 0), axis=1, keepdims=True
    )
    slot_row = jnp.sum(jnp.where(diagonal, slot_col, 0), axis=0, keepdims=True)
    shift = adapters.bit_length() - 1
    owner_row = lax.shift_right_logical(slot_row, shift)
    owner_col = lax.shift_right_logical(slot_col, shift)
    same = owner_col == owner_row
    rank_row = jnp.sum(
        jnp.where(same & (first_index < second_index), 1, 0), axis=0, keepdims=True
    )
    rank_col = jnp.sum(
        jnp.where(same & (second_index < first_index), 1, 0), axis=1, keepdims=True
    )
    target_row = owner_row * CAPACITY + rank_row
    target_col = owner_col * CAPACITY + rank_col
    tags = jnp.broadcast_to(
        (slot_col - owner_col * adapters).astype(jnp.float32), (rows, D)
    ).astype(jnp.bfloat16)

    loads[0].wait()
    for load in loads[2:7]:
        load.start()
    for b in range(4):
        piece = slots // 4
        placement = jnp.where(
            iota((piece, rows), 0) + b * piece == target_row, 1.0, 0.0
        ).astype(jnp.bfloat16)
        where = pl.ds(b * piece, piece)
        sent[where, width:] = jnp.dot(
            placement, tags, preferred_element_type=jnp.float32
        ).astype(jnp.bfloat16)

        def dispatch(c, carry, placement=placement, where=where):
            at = pl.ds(pl.multiple_of(c * 512, 512), 512)
            sent[where, at] = jnp.dot(
                placement, hidden[:, at], preferred_element_type=jnp.float32
            ).astype(jnp.bfloat16)
            return carry

        lax.fori_loop(0, width // 512, dispatch, 0)

    pl.semaphore_wait(barrier, len(OFFSETS) - 1 + 3)

    def rows_of(index):
        return pl.ds(pl.multiple_of(index * CAPACITY, CAPACITY), CAPACITY)

    row_copies = [None]
    for i, o in enumerate(OFFSETS):
        if i == 0:
            continue
        to = ahead(o)
        copy = pltpu.make_async_remote_copy(
            src_ref=sent.at[rows_of(to)],
            dst_ref=arrived.at[rows_of(i)],
            send_sem=row_send.at[i],
            recv_sem=row_recv.at[i],
            device_id={"dp": to},
            device_id_type=MESH,
        )
        copy.start()
        row_copies.append(copy)
    arrived[rows_of(0)] = sent[rows_of(me)]

    loads[1].wait()
    loads[9].wait()
    for d in range(owners):
        for m in range(MCAP):
            leaving[d * MCAP + m] = ext[handover[m, d]]

    page_copies = [None]
    for o in OFFSETS[1:]:
        to = ahead(o)
        i = len(page_copies)
        copy = pltpu.make_async_remote_copy(
            src_ref=leaving.at[pl.ds(to * MCAP, MCAP)],
            dst_ref=landing.at[pl.ds(me * MCAP, MCAP)],
            send_sem=page_send.at[i],
            recv_sem=page_recv.at[i],
            device_id={"dp": to},
            device_id_type=MESH,
        )
        copy.start()
        page_copies.append(copy)
    landing[pl.ds(me * MCAP, MCAP)] = leaving[pl.ds(me * MCAP, MCAP)]

    lane = iota((block, D), 1)
    left = lane < rank

    def wanted(b):
        tag = arrived[pl.ds(b * block, block), width:].astype(jnp.float32)
        return tag - jnp.where(left, 0.0, 1.0)

    def project(b):
        for i in range(b * group_devices, (b + 1) * group_devices):
            if i:
                row_copies[i].wait_recv()
        if b == 0:
            loads[2].wait()
        want = wanted(b)
        low[...] = jnp.zeros_like(low)

        def four(q, carry):
            x = arrived[pl.ds(b * block, block), :width]
            match = (q * 4).astype(jnp.float32)
            for j in range(3):
                weight = down[pl.ds(q * 4, 4), j].reshape(4 * rank, width)
                got = lax.dot_general(
                    x, weight, (((1,), (1,)), ((), ())), preferred_element_type=jnp.float32
                )
                low[j] += jnp.where(want == match, got[:, :D], 0.0) + jnp.where(
                    want == match + 2.0, got[:, D:], 0.0
                )
            return carry

        lax.fori_loop(0, adapters // 4, four, 0)
        both = [low[j] + pltpu.roll(low[j], rank, 1) for j in range(3)]
        part[b, :block] = jnp.where(left, both[0], both[1])
        part[b, block:] = jnp.where(
            left[:half_block], both[2][:half_block], both[2][half_block:]
        )
        copies = []
        for step in range(1, 4):
            copy = pltpu.make_async_remote_copy(
                src_ref=part.at[b],
                dst_ref=gathered.at[b, step - 1],
                send_sem=sum_send.at[b, step - 1],
                recv_sem=sum_recv.at[b, step - 1],
                device_id={"mp": (mine + step) % 4},
                device_id_type=MESH,
            )
            copy.start()
            copies.append(copy)
        return copies

    def back_copy(i, head):
        to = behind(OFFSETS[i])
        columns = pl.ds(head * chunk, chunk)
        return pltpu.make_async_remote_copy(
            src_ref=delta.at[rows_of(i), columns],
            dst_ref=back.at[rows_of(me), columns],
            send_sem=back_send.at[head, i],
            recv_sem=back_recv.at[head, i],
            device_id={"dp": to},
            device_id_type=MESH,
        )

    back_copies = {}

    def raise_up(b, copies):
        for copy in copies:
            copy.wait_recv()
        if b == 0:
            loads[3].wait()
            loads[4].wait()
        summed = (part[b] + gathered[b, 0]) + (gathered[b, 1] + gathered[b, 2])
        summed = summed.astype(jnp.bfloat16).astype(jnp.float32)
        first, second = summed[:block], summed[block:]
        first_turned = pltpu.roll(first, rank, 1)
        second_turned = pltpu.roll(second, rank, 1)
        half_left = left[:half_block]
        parts = [
            jnp.where(left, first, first_turned),
            jnp.where(left, first_turned, first),
            jnp.concatenate(
                [
                    jnp.where(half_left, second, second_turned),
                    jnp.where(half_left, second_turned, second),
                ],
                axis=0,
            ),
        ]
        want = wanted(b)
        spread = [
            jnp.concatenate(
                [
                    jnp.where(want == float(2 * p), one, 0.0).astype(jnp.bfloat16)
                    for p in range(adapters // 2)
                ],
                axis=1,
            )
            for one in parts
        ]
        here = pl.ds(b * block, block)
        depth = adapters * rank
        for head in range(kv_heads):
            start = head * per_head * D
            for c in range(0, per_head * D, 512):
                got = jnp.dot(
                    spread[0],
                    query_up[:, :, start + c : start + c + 512].reshape(depth, 512),
                    preferred_element_type=jnp.float32,
                )
                delta[here, head * chunk + c : head * chunk + c + 512] = (
                    adapter_scale * got
                ).astype(jnp.bfloat16)
        for j in range(2):
            got = jnp.dot(
                spread[1 + j],
                kv_up[:, j].reshape(depth, kv_heads * D),
                preferred_element_type=jnp.float32,
            )
            got = (adapter_scale * got).astype(jnp.bfloat16)
            for head in range(kv_heads):
                at = head * chunk + (per_head + j) * D
                delta[here, at : at + D] = got[:, head * D : (head + 1) * D]
        for head, which in SENDS[b]:
            for i in range(which * group_devices, (which + 1) * group_devices):
                if i == 0:
                    continue
                back_copies[head, i] = back_copy(i, head)
                back_copies[head, i].start()
        if b == 0:
            back[rows_of(me)] = delta[rows_of(0)]

    pending = None
    for b in range(blocks):
        started = project(b)
        if pending is not None:
            raise_up(b - 1, pending)
        pending = started
        if b == 0:
            sums = []
        sums.append(started)
    raise_up(blocks - 1, pending)

    for k in (5, 6, 10, 11):
        loads[k].wait()
    for k in range(2):
        base_new[:, k * kv_heads * D : (k + 1) * kv_heads * D] = base_kv[:, k, :].astype(
            jnp.float32
        )
    for i in range(1, len(OFFSETS)):
        page_copies[i].wait_recv()
    ext[pages:] = landing[...]

    pick = jnp.where(iota((rows, slots), 1) == target_col, 1.0, 0.0).astype(jnp.bfloat16)
    tokens = page_count * PAGE_TOKENS
    token = iota((per_head, tokens), 1)
    scale = D**-0.5

    def store(head):
        columns = pl.ds(head * per_head * D, per_head * D)
        return pltpu.make_async_copy(
            out_ref.at[:, columns], out_hbm.at[:, columns], load_sem.at[12 + head]
        )

    for head in range(kv_heads):
        for i in range(1, len(OFFSETS)):
            back_copies[head, i].wait_recv()
        for g in range(0, per_head + 2, 2):
            got = jnp.dot(
                pick,
                back[:, head * chunk + g * D : head * chunk + (g + 2) * D],
                preferred_element_type=jnp.float32,
            )
            for k in range(2):
                one = got[:, k * D : (k + 1) * D]
                if g < per_head:
                    at = (head * per_head + g + k) * D
                    base = base_query[:, at : at + D]
                else:
                    at = (k * kv_heads + head) * D
                    base = base_new[:, at : at + D]
                value = (base.astype(jnp.float32) + one).astype(jnp.bfloat16).astype(jnp.float32)
                if g < per_head:
                    wide[:, g + k, :] = value
                else:
                    fresh[:, k * D : (k + 1) * D] = value

        def gather(r, which, head=head):
            return jnp.concatenate(
                [
                    ext[table[p, r], which, :, head * D : (head + 1) * D]
                    for p in range(page_count)
                ],
                axis=0,
            )

        def score(r, gather=gather):
            return lax.dot_general(
                wide[r].astype(jnp.bfloat16),
                gather(r, 0),
                (((1,), (1,)), ((), ())),
                preferred_element_type=jnp.float32,
            )

        def soft(r, s):
            s = jnp.where(token < lens[0, r], s * scale, -jnp.inf)
            new = fresh[pl.ds(r, 1), :]
            own = jnp.sum(wide[r] * new[:, :D], axis=1, keepdims=True) * scale
            top = jnp.maximum(jnp.max(s, axis=1, keepdims=True), own)
            p = jnp.exp(s - top)
            po = jnp.exp(own - top)
            inv = 1.0 / (jnp.sum(p, axis=1, keepdims=True) + po)
            own_part = (po * inv).astype(jnp.bfloat16).astype(jnp.float32) * new[:, D:]
            return (p * inv).astype(jnp.bfloat16), own_part

        def weigh(r, p, own_part, gather=gather):
            wide[r] = jnp.dot(p, gather(r, 1), preferred_element_type=jnp.float32) + own_part

        def body(i, carry):
            at = i * GROUP
            scores = [score(at + j) for j in range(GROUP)]
            weights = [soft(at + j, scores[j]) for j in range(GROUP)]
            for j in range(GROUP):
                weigh(at + j, *weights[j])
            return carry

        lax.fori_loop(0, rows // GROUP, body, 0)
        for g in range(per_head):
            at = (head * per_head + g) * D
            out_ref[:, at : at + D] = wide[:, g, :].astype(jnp.bfloat16)
        store(head).start()

    for i in range(1, len(OFFSETS)):
        row_copies[i].wait_send()
        page_copies[i].wait_send()
        for head in range(kv_heads):
            back_copies[head, i].wait_send()
    for copies in sums:
        for copy in copies:
            copy.wait_send()
    for head in range(kv_heads):
        store(head).wait()


def shards(
    hidden,
    base_query_rows,
    key_value_base,
    key_value_pool,
    request_page_table,
    context_length,
    handover_pages,
    request_adapter,
    adapter_position,
    adapter_down_weight,
    query_up_weight,
    key_value_up,
):
    rows, width = hidden.shape
    owners = handover_pages.shape[0]
    slots = owners * CAPACITY
    query_part = base_query_rows.shape[1]
    kv_part = key_value_base.shape[2]
    kv_heads = kv_part // HEAD_SIZE
    per_head = query_part // kv_part
    total = adapter_position.shape[0]
    rank = adapter_down_weight.shape[2]
    blocks = 4
    block = slots // blocks
    packed = block * 3 // 2
    pages = key_value_pool.shape[0]
    bf16, f32 = jnp.bfloat16, jnp.float32
    hbm = pl.BlockSpec(memory_space=pl.ANY)
    dma = pltpu.SemaphoreType.DMA
    return pl.pallas_call(
        fused,
        out_shape=jax.ShapeDtypeStruct((rows, query_part), bf16),
        in_specs=[hbm] * 12,
        out_specs=hbm,
        scratch_shapes=[
            pltpu.VMEM((1, rows), jnp.int32),
            pltpu.VMEM((1, total), jnp.int32),
            pltpu.SMEM(request_page_table.shape[::-1], jnp.int32),
            pltpu.SMEM((1, rows), jnp.int32),
            pltpu.SMEM(handover_pages.shape[::-1], jnp.int32),
            pltpu.VMEM((rows, query_part), bf16),
            pltpu.VMEM((rows, width), bf16),
            pltpu.VMEM((rows, query_part), bf16),
            pltpu.VMEM(key_value_base.shape, bf16),
            pltpu.VMEM((rows, 2 * kv_part), f32),
            pltpu.VMEM(adapter_down_weight.shape, bf16),
            pltpu.VMEM(query_up_weight.shape, bf16),
            pltpu.VMEM(key_value_up.shape, bf16),
            pltpu.VMEM((slots, width + HEAD_SIZE), bf16),
            pltpu.VMEM((slots, width + HEAD_SIZE), bf16),
            pltpu.VMEM((owners * MCAP,) + key_value_pool.shape[1:], bf16),
            pltpu.VMEM((owners * MCAP,) + key_value_pool.shape[1:], bf16),
            pltpu.VMEM((pages + owners * MCAP,) + key_value_pool.shape[1:], bf16),
            pltpu.VMEM((3, block, HEAD_SIZE), f32),
            pltpu.VMEM((blocks, packed, HEAD_SIZE), f32),
            pltpu.VMEM((blocks, 3, packed, HEAD_SIZE), f32),
            pltpu.VMEM((slots, query_part + 2 * kv_part), bf16),
            pltpu.VMEM((slots, query_part + 2 * kv_part), bf16),
            pltpu.VMEM((rows, per_head, HEAD_SIZE), f32),
            pltpu.VMEM((rows, 2 * HEAD_SIZE), f32),
            dma((12 + kv_heads,)),
            dma((owners,)),
            dma((owners,)),
            dma((owners,)),
            dma((owners,)),
            dma((blocks, 3)),
            dma((blocks, 3)),
            dma((kv_heads, owners)),
            dma((kv_heads, owners)),
        ],
        compiler_params=pltpu.CompilerParams(
            collective_id=0, has_side_effects=True, vmem_limit_bytes=56 * 1024 * 1024
        ),
    )(
        request_adapter.reshape(1, rows),
        adapter_position.reshape(1, total),
        request_page_table.T,
        context_length.reshape(1, rows),
        handover_pages.T,
        hidden,
        base_query_rows,
        key_value_base,
        key_value_pool,
        adapter_down_weight,
        query_up_weight,
        key_value_up,
    )


def solution(mesh):
    return jax.shard_map(
        shards,
        mesh=mesh,
        in_specs=(
            P("dp", "mp"),
            P("dp", "mp"),
            P("dp", None, "mp"),
            P("dp", None, None, "mp"),
            P("dp", None),
            P("dp"),
            P("dp", None),
            P("dp"),
            P(),
            P("dp", None, None, "mp"),
            P("dp", None, "mp"),
            P("dp", None, None, "mp"),
        ),
        out_specs=P("dp", "mp"),
        check_vma=False,
    )
```

```python
import jax
import jax.numpy as jnp
from jax import lax
from jax.experimental import pallas as pl
from jax.experimental.pallas import tpu as pltpu
from jax.sharding import PartitionSpec as P

HEAD_SIZE = 128
PAGE_TOKENS = 16
MCAP = 2
CAPACITY = 16
GROUP = 16
MESH = pl.DeviceIdType.MESH

adapter_scale = 0.5


def torus_offsets():
    near = [(1, 0), (0, 1), (3, 0), (0, 3)]
    diagonal = [(1, 1), (3, 3), (1, 3), (3, 1)]
    bent = [(2, 1), (1, 2), (2, 3), (3, 2)]
    straight = [(2, 0), (0, 2)]
    order = [(0, 0, 0), (0, 0, 1)]
    for chips in (near, diagonal, bent, straight, [(2, 2)]):
        for core in (0, 1):
            order += [(y, z, core) for y, z in chips]
    return order


OFFSETS = torus_offsets()
SENDS = [[(0, 0)], [(0, 1)], [(0, 2), (1, 0), (1, 1)], [(0, 3), (1, 2), (1, 3)]]


def fused(
    ids_hbm,
    place_hbm,
    table_hbm,
    lens_hbm,
    handover_hbm,
    hidden_hbm,
    base_query_hbm,
    base_kv_hbm,
    pool_hbm,
    down_hbm,
    query_up_hbm,
    kv_up_hbm,
    out_hbm,
    ids_row,
    place_row,
    table,
    lens,
    handover,
    out_ref,
    hidden,
    base_query,
    base_kv,
    base_new,
    down,
    query_up,
    kv_up,
    sent,
    arrived,
    leaving,
    landing,
    ext,
    low,
    part,
    gathered,
    delta,
    back,
    wide,
    fresh,
    load_sem,
    row_send,
    row_recv,
    page_send,
    page_recv,
    sum_send,
    sum_recv,
    back_send,
    back_recv,
):
    rows, width = hidden.shape
    slots = arrived.shape[0]
    owners = slots // CAPACITY
    adapters, _, rank, _ = down.shape
    pages = pool_hbm.shape[0]
    page_count = table.shape[0]
    D = HEAD_SIZE
    kv_heads = base_kv.shape[2] // D
    per_head = base_query.shape[1] // (kv_heads * D)
    chunk = (per_head + 2) * D
    blocks, packed = part.shape[0], part.shape[1]
    block = slots // blocks
    half_block = block // 2
    group_devices = block // CAPACITY

    loads = [
        pltpu.make_async_copy(hidden_hbm, hidden, load_sem.at[0]),
        pltpu.make_async_copy(pool_hbm, ext.at[pl.ds(0, pages)], load_sem.at[1]),
        pltpu.make_async_copy(down_hbm, down, load_sem.at[2]),
        pltpu.make_async_copy(query_up_hbm, query_up, load_sem.at[3]),
        pltpu.make_async_copy(kv_up_hbm, kv_up, load_sem.at[4]),
        pltpu.make_async_copy(base_query_hbm, base_query, load_sem.at[5]),
        pltpu.make_async_copy(base_kv_hbm, base_kv, load_sem.at[6]),
        pltpu.make_async_copy(ids_hbm, ids_row, load_sem.at[7]),
        pltpu.make_async_copy(place_hbm, place_row, load_sem.at[8]),
        pltpu.make_async_copy(handover_hbm, handover, load_sem.at[9]),
        pltpu.make_async_copy(table_hbm, table, load_sem.at[10]),
        pltpu.make_async_copy(lens_hbm, lens, load_sem.at[11]),
    ]
    for k in (7, 8, 0, 9, 1, 10, 11):
        loads[k].start()

    me = lax.axis_index("dp")
    mine = lax.axis_index("mp")
    y, z, core = me // 8, (me // 2) % 4, me % 2

    def ahead(o):
        return ((y + o[0]) % 4) * 8 + ((z + o[1]) % 4) * 2 + (core + o[2]) % 2

    def behind(o):
        return ((y + 4 - o[0]) % 4) * 8 + ((z + 4 - o[1]) % 4) * 2 + (core + o[2]) % 2

    def iota(shape, axis):
        return lax.broadcasted_iota(jnp.int32, shape, axis)

    barrier = pltpu.get_barrier_semaphore()
    for o in OFFSETS[1:]:
        pl.semaphore_signal(barrier, inc=1, device_id={"dp": ahead(o)}, device_id_type=MESH)
    for step in range(1, 4):
        pl.semaphore_signal(
            barrier, inc=1, device_id={"mp": (mine + step) % 4}, device_id_type=MESH
        )

    loads[7].wait()
    loads[8].wait()
    total = place_row.shape[1]
    first_index, second_index = iota((rows, rows), 0), iota((rows, rows), 1)
    diagonal = first_index == second_index
    ids_col = jnp.sum(jnp.where(diagonal, ids_row[...], 0), axis=1, keepdims=True)
    slot_col = jnp.sum(
        jnp.where(iota((rows, total), 1) == ids_col, place_row[...], 0), axis=1, keepdims=True
    )
    slot_row = jnp.sum(jnp.where(diagonal, slot_col, 0), axis=0, keepdims=True)
    shift = adapters.bit_length() - 1
    owner_row = lax.shift_right_logical(slot_row, shift)
    owner_col = lax.shift_right_logical(slot_col, shift)
    same = owner_col == owner_row
    rank_row = jnp.sum(
        jnp.where(same & (first_index < second_index), 1, 0), axis=0, keepdims=True
    )
    rank_col = jnp.sum(
        jnp.where(same & (second_index < first_index), 1, 0), axis=1, keepdims=True
    )
    target_row = owner_row * CAPACITY + rank_row
    target_col = owner_col * CAPACITY + rank_col
    tags = jnp.broadcast_to(
        (slot_col - owner_col * adapters).astype(jnp.float32), (rows, D)
    ).astype(jnp.bfloat16)

    loads[0].wait()
    for load in loads[2:7]:
        load.start()
    for b in range(4):
        piece = slots // 4
        placement = jnp.where(
            iota((piece, rows), 0) + b * piece == target_row, 1.0, 0.0
        ).astype(jnp.bfloat16)
        where = pl.ds(b * piece, piece)
        sent[where, width:] = jnp.dot(
            placement, tags, preferred_element_type=jnp.float32
        ).astype(jnp.bfloat16)

        def dispatch(c, carry, placement=placement, where=where):
            at = pl.ds(pl.multiple_of(c * 512, 512), 512)
            sent[where, at] = jnp.dot(
                placement, hidden[:, at], preferred_element_type=jnp.float32
            ).astype(jnp.bfloat16)
            return carry

        lax.fori_loop(0, width // 512, dispatch, 0)

    pl.semaphore_wait(barrier, len(OFFSETS) - 1 + 3)

    def rows_of(index):
        return pl.ds(pl.multiple_of(index * CAPACITY, CAPACITY), CAPACITY)

    row_copies = [None]
    for i, o in enumerate(OFFSETS):
        if i == 0:
            continue
        to = ahead(o)
        copy = pltpu.make_async_remote_copy(
            src_ref=sent.at[rows_of(to)],
            dst_ref=arrived.at[rows_of(i)],
            send_sem=row_send.at[i],
            recv_sem=row_recv.at[i],
            device_id={"dp": to},
            device_id_type=MESH,
        )
        copy.start()
        row_copies.append(copy)
    arrived[rows_of(0)] = sent[rows_of(me)]

    loads[1].wait()
    loads[9].wait()
    for d in range(owners):
        for m in range(MCAP):
            leaving[d * MCAP + m] = ext[handover[m, d]]

    page_copies = [None]
    for o in OFFSETS[1:]:
        to = ahead(o)
        i = len(page_copies)
        copy = pltpu.make_async_remote_copy(
            src_ref=leaving.at[pl.ds(to * MCAP, MCAP)],
            dst_ref=landing.at[pl.ds(me * MCAP, MCAP)],
            send_sem=page_send.at[i],
            recv_sem=page_recv.at[i],
            device_id={"dp": to},
            device_id_type=MESH,
        )
        copy.start()
        page_copies.append(copy)
    landing[pl.ds(me * MCAP, MCAP)] = leaving[pl.ds(me * MCAP, MCAP)]

    lane = iota((block, D), 1)
    left = lane < rank

    def wanted(b):
        tag = arrived[pl.ds(b * block, block), width:].astype(jnp.float32)
        return tag - jnp.where(left, 0.0, 1.0)

    def project(b):
        for i in range(b * group_devices, (b + 1) * group_devices):
            if i:
                row_copies[i].wait_recv()
        if b == 0:
            loads[2].wait()
        want = wanted(b)
        low[...] = jnp.zeros_like(low)

        def four(q, carry):
            x = arrived[pl.ds(b * block, block), :width]
            match = (q * 4).astype(jnp.float32)
            for j in range(3):
                weight = down[pl.ds(q * 4, 4), j].reshape(4 * rank, width)
                got = lax.dot_general(
                    x, weight, (((1,), (1,)), ((), ())), preferred_element_type=jnp.float32
                )
                low[j] += jnp.where(want == match, got[:, :D], 0.0) + jnp.where(
                    want == match + 2.0, got[:, D:], 0.0
                )
            return carry

        lax.fori_loop(0, adapters // 4, four, 0)
        both = [low[j] + pltpu.roll(low[j], rank, 1) for j in range(3)]
        part[b, :block] = jnp.where(left, both[0], both[1])
        part[b, block:] = jnp.where(
            left[:half_block], both[2][:half_block], both[2][half_block:]
        )
        copies = []
        for step in range(1, 4):
            copy = pltpu.make_async_remote_copy(
                src_ref=part.at[b],
                dst_ref=gathered.at[b, step - 1],
                send_sem=sum_send.at[b, step - 1],
                recv_sem=sum_recv.at[b, step - 1],
                device_id={"mp": (mine + step) % 4},
                device_id_type=MESH,
            )
            copy.start()
            copies.append(copy)
        return copies

    def back_copy(i, head):
        to = behind(OFFSETS[i])
        columns = pl.ds(head * chunk, chunk)
        return pltpu.make_async_remote_copy(
            src_ref=delta.at[rows_of(i), columns],
            dst_ref=back.at[rows_of(me), columns],
            send_sem=back_send.at[head, i],
            recv_sem=back_recv.at[head, i],
            device_id={"dp": to},
            device_id_type=MESH,
        )

    back_copies = {}

    def raise_up(b, copies):
        for copy in copies:
            copy.wait_recv()
        if b == 0:
            loads[3].wait()
            loads[4].wait()
        summed = (part[b] + gathered[b, 0]) + (gathered[b, 1] + gathered[b, 2])
        summed = summed.astype(jnp.bfloat16).astype(jnp.float32)
        first, second = summed[:block], summed[block:]
        first_turned = pltpu.roll(first, rank, 1)
        second_turned = pltpu.roll(second, rank, 1)
        half_left = left[:half_block]
        parts = [
            jnp.where(left, first, first_turned),
            jnp.where(left, first_turned, first),
            jnp.concatenate(
                [
                    jnp.where(half_left, second, second_turned),
                    jnp.where(half_left, second_turned, second),
                ],
                axis=0,
            ),
        ]
        want = wanted(b)
        spread = [
            jnp.concatenate(
                [
                    jnp.where(want == float(2 * p), one, 0.0).astype(jnp.bfloat16)
                    for p in range(adapters // 2)
                ],
                axis=1,
            )
            for one in parts
        ]
        here = pl.ds(b * block, block)
        depth = adapters * rank
        for head in range(kv_heads):
            start = head * per_head * D
            for c in range(0, per_head * D, 512):
                got = jnp.dot(
                    spread[0],
                    query_up[:, :, start + c : start + c + 512].reshape(depth, 512),
                    preferred_element_type=jnp.float32,
                )
                delta[here, head * chunk + c : head * chunk + c + 512] = (
                    adapter_scale * got
                ).astype(jnp.bfloat16)
        for j in range(2):
            got = jnp.dot(
                spread[1 + j],
                kv_up[:, j].reshape(depth, kv_heads * D),
                preferred_element_type=jnp.float32,
            )
            got = (adapter_scale * got).astype(jnp.bfloat16)
            for head in range(kv_heads):
                at = head * chunk + (per_head + j) * D
                delta[here, at : at + D] = got[:, head * D : (head + 1) * D]
        for head, which in SENDS[b]:
            for i in range(which * group_devices, (which + 1) * group_devices):
                if i == 0:
                    continue
                back_copies[head, i] = back_copy(i, head)
                back_copies[head, i].start()
        if b == 0:
            back[rows_of(me)] = delta[rows_of(0)]

    pending = None
    for b in range(blocks):
        started = project(b)
        if pending is not None:
            raise_up(b - 1, pending)
        pending = started
        if b == 0:
            sums = []
        sums.append(started)
    raise_up(blocks - 1, pending)

    for k in (5, 6, 10, 11):
        loads[k].wait()
    for k in range(2):
        base_new[:, k * kv_heads * D : (k + 1) * kv_heads * D] = base_kv[:, k, :].astype(
            jnp.float32
        )
    for i in range(1, len(OFFSETS)):
        page_copies[i].wait_recv()
    ext[pages:] = landing[...]

    pick = jnp.where(iota((rows, slots), 1) == target_col, 1.0, 0.0).astype(jnp.bfloat16)
    tokens = page_count * PAGE_TOKENS
    heads = kv_heads * per_head
    token = iota((heads, tokens), 1)
    upper = iota((heads, D), 0) < per_head
    scale = D**-0.5

    def store(head):
        columns = pl.ds(head * per_head * D, per_head * D)
        return pltpu.make_async_copy(
            out_ref.at[:, columns], out_hbm.at[:, columns], load_sem.at[12 + head]
        )

    for head in range(kv_heads):
        for i in range(1, len(OFFSETS)):
            back_copies[head, i].wait_recv()
        for g in range(0, per_head + 2, 2):
            got = jnp.dot(
                pick,
                back[:, head * chunk + g * D : head * chunk + (g + 2) * D],
                preferred_element_type=jnp.float32,
            )
            for k in range(2):
                one = got[:, k * D : (k + 1) * D]
                if g < per_head:
                    at = (head * per_head + g + k) * D
                    base = base_query[:, at : at + D]
                else:
                    at = (k * kv_heads + head) * D
                    base = base_new[:, at : at + D]
                value = (base.astype(jnp.float32) + one).astype(jnp.bfloat16).astype(jnp.float32)
                if g < per_head:
                    wide[:, head * per_head + g + k, :] = value
                else:
                    fresh[:, at : at + D] = value

    def gather(r, which):
        return jnp.concatenate([ext[table[p, r], which] for p in range(page_count)], axis=0)

    def per_row(r, at):
        new = fresh[pl.ds(r, 1), at : at + 2 * D]
        return jnp.concatenate(
            [
                jnp.broadcast_to(new[:, :D], (per_head, D)),
                jnp.broadcast_to(new[:, D:], (per_head, D)),
            ],
            axis=0,
        )

    def score(r):
        q = wide[r]
        zero = jnp.zeros_like(q)
        both = jnp.concatenate(
            [jnp.where(upper, q, zero), jnp.where(upper, zero, q)], axis=1
        ).astype(jnp.bfloat16)
        return lax.dot_general(
            both, gather(r, 0), (((1,), (1,)), ((), ())), preferred_element_type=jnp.float32
        )

    def soft(r, s):
        s = jnp.where(token < lens[0, r], s * scale, -jnp.inf)
        own = jnp.sum(wide[r] * per_row(r, 0), axis=1, keepdims=True) * scale
        top = jnp.maximum(jnp.max(s, axis=1, keepdims=True), own)
        p = jnp.exp(s - top)
        po = jnp.exp(own - top)
        inv = 1.0 / (jnp.sum(p, axis=1, keepdims=True) + po)
        own_weight = (po * inv).astype(jnp.bfloat16).astype(jnp.float32)
        return (p * inv).astype(jnp.bfloat16), own_weight * per_row(r, 2 * D)

    def weigh(r, p, own_part):
        o = jnp.dot(p, gather(r, 1), preferred_element_type=jnp.float32)
        wide[r] = jnp.where(upper, o[:, :D], o[:, D:]) + own_part

    def body(i, carry):
        at = i * GROUP
        scores = [score(at + j) for j in range(GROUP)]
        weights = [soft(at + j, scores[j]) for j in range(GROUP)]
        for j in range(GROUP):
            weigh(at + j, *weights[j])
        return carry

    lax.fori_loop(0, rows // GROUP, body, 0)
    for head in range(kv_heads):
        for g in range(per_head):
            at = (head * per_head + g) * D
            out_ref[:, at : at + D] = wide[:, head * per_head + g, :].astype(jnp.bfloat16)
        store(head).start()

    for i in range(1, len(OFFSETS)):
        row_copies[i].wait_send()
        page_copies[i].wait_send()
        for head in range(kv_heads):
            back_copies[head, i].wait_send()
    for copies in sums:
        for copy in copies:
            copy.wait_send()
    for head in range(kv_heads):
        store(head).wait()


def shards(
    hidden,
    base_query_rows,
    key_value_base,
    key_value_pool,
    request_page_table,
    context_length,
    handover_pages,
    request_adapter,
    adapter_position,
    adapter_down_weight,
    query_up_weight,
    key_value_up,
):
    rows, width = hidden.shape
    owners = handover_pages.shape[0]
    slots = owners * CAPACITY
    query_part = base_query_rows.shape[1]
    kv_part = key_value_base.shape[2]
    kv_heads = kv_part // HEAD_SIZE
    per_head = query_part // kv_part
    total = adapter_position.shape[0]
    rank = adapter_down_weight.shape[2]
    blocks = 4
    block = slots // blocks
    packed = block * 3 // 2
    pages = key_value_pool.shape[0]
    bf16, f32 = jnp.bfloat16, jnp.float32
    hbm = pl.BlockSpec(memory_space=pl.ANY)
    dma = pltpu.SemaphoreType.DMA
    return pl.pallas_call(
        fused,
        out_shape=jax.ShapeDtypeStruct((rows, query_part), bf16),
        in_specs=[hbm] * 12,
        out_specs=hbm,
        scratch_shapes=[
            pltpu.VMEM((1, rows), jnp.int32),
            pltpu.VMEM((1, total), jnp.int32),
            pltpu.SMEM(request_page_table.shape[::-1], jnp.int32),
            pltpu.SMEM((1, rows), jnp.int32),
            pltpu.SMEM(handover_pages.shape[::-1], jnp.int32),
            pltpu.VMEM((rows, query_part), bf16),
            pltpu.VMEM((rows, width), bf16),
            pltpu.VMEM((rows, query_part), bf16),
            pltpu.VMEM(key_value_base.shape, bf16),
            pltpu.VMEM((rows, 2 * kv_part), f32),
            pltpu.VMEM(adapter_down_weight.shape, bf16),
            pltpu.VMEM(query_up_weight.shape, bf16),
            pltpu.VMEM(key_value_up.shape, bf16),
            pltpu.VMEM((slots, width + HEAD_SIZE), bf16),
            pltpu.VMEM((slots, width + HEAD_SIZE), bf16),
            pltpu.VMEM((owners * MCAP,) + key_value_pool.shape[1:], bf16),
            pltpu.VMEM((owners * MCAP,) + key_value_pool.shape[1:], bf16),
            pltpu.VMEM((pages + owners * MCAP,) + key_value_pool.shape[1:], bf16),
            pltpu.VMEM((3, block, HEAD_SIZE), f32),
            pltpu.VMEM((blocks, packed, HEAD_SIZE), f32),
            pltpu.VMEM((blocks, 3, packed, HEAD_SIZE), f32),
            pltpu.VMEM((slots, query_part + 2 * kv_part), bf16),
            pltpu.VMEM((slots, query_part + 2 * kv_part), bf16),
            pltpu.VMEM((rows, kv_heads * per_head, HEAD_SIZE), f32),
            pltpu.VMEM((rows, 2 * kv_part), f32),
            dma((12 + kv_heads,)),
            dma((owners,)),
            dma((owners,)),
            dma((owners,)),
            dma((owners,)),
            dma((blocks, 3)),
            dma((blocks, 3)),
            dma((kv_heads, owners)),
            dma((kv_heads, owners)),
        ],
        compiler_params=pltpu.CompilerParams(
            collective_id=0, has_side_effects=True, vmem_limit_bytes=56 * 1024 * 1024
        ),
    )(
        request_adapter.reshape(1, rows),
        adapter_position.reshape(1, total),
        request_page_table.T,
        context_length.reshape(1, rows),
        handover_pages.T,
        hidden,
        base_query_rows,
        key_value_base,
        key_value_pool,
        adapter_down_weight,
        query_up_weight,
        key_value_up,
    )


def solution(mesh):
    return jax.shard_map(
        shards,
        mesh=mesh,
        in_specs=(
            P("dp", "mp"),
            P("dp", "mp"),
            P("dp", None, "mp"),
            P("dp", None, None, "mp"),
            P("dp", None),
            P("dp"),
            P("dp", None),
            P("dp"),
            P(),
            P("dp", None, None, "mp"),
            P("dp", None, "mp"),
            P("dp", None, None, "mp"),
        ),
        out_specs=P("dp", "mp"),
        check_vma=False,
    )
```

```python
import jax
import jax.numpy as jnp
from jax import lax
from jax.experimental import pallas as pl
from jax.experimental.pallas import tpu as pltpu
from jax.sharding import PartitionSpec as P

HEAD_SIZE = 128
PAGE_TOKENS = 16
MCAP = 2
CAPACITY = 16
GROUP = 32
MESH = pl.DeviceIdType.MESH

adapter_scale = 0.5


def torus_offsets():
    near = [(1, 0), (0, 1), (3, 0), (0, 3)]
    diagonal = [(1, 1), (3, 3), (1, 3), (3, 1)]
    bent = [(2, 1), (1, 2), (2, 3), (3, 2)]
    straight = [(2, 0), (0, 2)]
    order = [(0, 0, 0), (0, 0, 1)]
    for chips in (near, diagonal, bent, straight, [(2, 2)]):
        for core in (0, 1):
            order += [(y, z, core) for y, z in chips]
    return order


OFFSETS = torus_offsets()
SENDS = [[(0, 0)], [(0, 1)], [(0, 2), (1, 0), (1, 1)], [(0, 3), (1, 2), (1, 3)]]


def fused(
    ids_hbm,
    place_hbm,
    table_hbm,
    lens_hbm,
    handover_hbm,
    hidden_hbm,
    base_query_hbm,
    base_kv_hbm,
    pool_hbm,
    down_hbm,
    query_up_hbm,
    kv_up_hbm,
    out_hbm,
    ids_row,
    place_row,
    table,
    lens,
    handover,
    out_ref,
    hidden,
    base_query,
    base_kv,
    base_new,
    down,
    query_up,
    kv_up,
    sent,
    arrived,
    leaving,
    landing,
    ext,
    low,
    part,
    gathered,
    delta,
    back,
    wide,
    fresh,
    load_sem,
    row_send,
    row_recv,
    page_send,
    page_recv,
    sum_send,
    sum_recv,
    back_send,
    back_recv,
):
    rows, width = hidden.shape
    slots = arrived.shape[0]
    owners = slots // CAPACITY
    adapters, _, rank, _ = down.shape
    pages = pool_hbm.shape[0]
    page_count = table.shape[0]
    D = HEAD_SIZE
    kv_heads = base_kv.shape[2] // D
    per_head = base_query.shape[1] // (kv_heads * D)
    chunk = (per_head + 2) * D
    blocks, packed = part.shape[0], part.shape[1]
    block = slots // blocks
    half_block = block // 2
    group_devices = block // CAPACITY

    loads = [
        pltpu.make_async_copy(hidden_hbm, hidden, load_sem.at[0]),
        pltpu.make_async_copy(pool_hbm, ext.at[pl.ds(0, pages)], load_sem.at[1]),
        pltpu.make_async_copy(down_hbm, down, load_sem.at[2]),
        pltpu.make_async_copy(query_up_hbm, query_up, load_sem.at[3]),
        pltpu.make_async_copy(kv_up_hbm, kv_up, load_sem.at[4]),
        pltpu.make_async_copy(base_query_hbm, base_query, load_sem.at[5]),
        pltpu.make_async_copy(base_kv_hbm, base_kv, load_sem.at[6]),
        pltpu.make_async_copy(ids_hbm, ids_row, load_sem.at[7]),
        pltpu.make_async_copy(place_hbm, place_row, load_sem.at[8]),
        pltpu.make_async_copy(handover_hbm, handover, load_sem.at[9]),
        pltpu.make_async_copy(table_hbm, table, load_sem.at[10]),
        pltpu.make_async_copy(lens_hbm, lens, load_sem.at[11]),
    ]
    for k in (7, 8, 0, 9, 1, 10, 11):
        loads[k].start()

    me = lax.axis_index("dp")
    mine = lax.axis_index("mp")
    y, z, core = me // 8, (me // 2) % 4, me % 2

    def ahead(o):
        return ((y + o[0]) % 4) * 8 + ((z + o[1]) % 4) * 2 + (core + o[2]) % 2

    def behind(o):
        return ((y + 4 - o[0]) % 4) * 8 + ((z + 4 - o[1]) % 4) * 2 + (core + o[2]) % 2

    def iota(shape, axis):
        return lax.broadcasted_iota(jnp.int32, shape, axis)

    barrier = pltpu.get_barrier_semaphore()
    for o in OFFSETS[1:]:
        pl.semaphore_signal(barrier, inc=1, device_id={"dp": ahead(o)}, device_id_type=MESH)
    for step in range(1, 4):
        pl.semaphore_signal(
            barrier, inc=1, device_id={"mp": (mine + step) % 4}, device_id_type=MESH
        )

    loads[7].wait()
    loads[8].wait()
    total = place_row.shape[1]
    first_index, second_index = iota((rows, rows), 0), iota((rows, rows), 1)
    diagonal = first_index == second_index
    ids_col = jnp.sum(jnp.where(diagonal, ids_row[...], 0), axis=1, keepdims=True)
    slot_col = jnp.sum(
        jnp.where(iota((rows, total), 1) == ids_col, place_row[...], 0), axis=1, keepdims=True
    )
    slot_row = jnp.sum(jnp.where(diagonal, slot_col, 0), axis=0, keepdims=True)
    shift = adapters.bit_length() - 1
    owner_row = lax.shift_right_logical(slot_row, shift)
    owner_col = lax.shift_right_logical(slot_col, shift)
    same = owner_col == owner_row
    rank_row = jnp.sum(
        jnp.where(same & (first_index < second_index), 1, 0), axis=0, keepdims=True
    )
    rank_col = jnp.sum(
        jnp.where(same & (second_index < first_index), 1, 0), axis=1, keepdims=True
    )
    target_row = owner_row * CAPACITY + rank_row
    target_col = owner_col * CAPACITY + rank_col
    tags = jnp.broadcast_to(
        (slot_col - owner_col * adapters).astype(jnp.float32), (rows, D)
    ).astype(jnp.bfloat16)

    loads[0].wait()
    for load in loads[2:7]:
        load.start()
    for b in range(4):
        piece = slots // 4
        placement = jnp.where(
            iota((piece, rows), 0) + b * piece == target_row, 1.0, 0.0
        ).astype(jnp.bfloat16)
        where = pl.ds(b * piece, piece)
        sent[where, width:] = jnp.dot(
            placement, tags, preferred_element_type=jnp.float32
        ).astype(jnp.bfloat16)

        def dispatch(c, carry, placement=placement, where=where):
            at = pl.ds(pl.multiple_of(c * 512, 512), 512)
            sent[where, at] = jnp.dot(
                placement, hidden[:, at], preferred_element_type=jnp.float32
            ).astype(jnp.bfloat16)
            return carry

        lax.fori_loop(0, width // 512, dispatch, 0)

    pl.semaphore_wait(barrier, len(OFFSETS) - 1 + 3)

    def rows_of(index):
        return pl.ds(pl.multiple_of(index * CAPACITY, CAPACITY), CAPACITY)

    row_copies = [None]
    for i, o in enumerate(OFFSETS):
        if i == 0:
            continue
        to = ahead(o)
        copy = pltpu.make_async_remote_copy(
            src_ref=sent.at[rows_of(to)],
            dst_ref=arrived.at[rows_of(i)],
            send_sem=row_send.at[i],
            recv_sem=row_recv.at[i],
            device_id={"dp": to},
            device_id_type=MESH,
        )
        copy.start()
        row_copies.append(copy)
    arrived[rows_of(0)] = sent[rows_of(me)]

    loads[1].wait()
    loads[9].wait()
    for d in range(owners):
        for m in range(MCAP):
            leaving[d * MCAP + m] = ext[handover[m, d]]

    page_copies = [None]
    for o in OFFSETS[1:]:
        to = ahead(o)
        i = len(page_copies)
        copy = pltpu.make_async_remote_copy(
            src_ref=leaving.at[pl.ds(to * MCAP, MCAP)],
            dst_ref=landing.at[pl.ds(me * MCAP, MCAP)],
            send_sem=page_send.at[i],
            recv_sem=page_recv.at[i],
            device_id={"dp": to},
            device_id_type=MESH,
        )
        copy.start()
        page_copies.append(copy)
    landing[pl.ds(me * MCAP, MCAP)] = leaving[pl.ds(me * MCAP, MCAP)]

    lane = iota((block, D), 1)
    left = lane < rank

    def wanted(b):
        tag = arrived[pl.ds(b * block, block), width:].astype(jnp.float32)
        return tag - jnp.where(left, 0.0, 1.0)

    def project(b):
        for i in range(b * group_devices, (b + 1) * group_devices):
            if i:
                row_copies[i].wait_recv()
        if b == 0:
            loads[2].wait()
        want = wanted(b)
        low[...] = jnp.zeros_like(low)

        def four(q, carry):
            x = arrived[pl.ds(b * block, block), :width]
            match = (q * 4).astype(jnp.float32)
            for j in range(3):
                weight = down[pl.ds(q * 4, 4), j].reshape(4 * rank, width)
                got = lax.dot_general(
                    x, weight, (((1,), (1,)), ((), ())), preferred_element_type=jnp.float32
                )
                low[j] += jnp.where(want == match, got[:, :D], 0.0) + jnp.where(
                    want == match + 2.0, got[:, D:], 0.0
                )
            return carry

        lax.fori_loop(0, adapters // 4, four, 0)
        both = [low[j] + pltpu.roll(low[j], rank, 1) for j in range(3)]
        part[b, :block] = jnp.where(left, both[0], both[1])
        part[b, block:] = jnp.where(
            left[:half_block], both[2][:half_block], both[2][half_block:]
        )
        copies = []
        for step in range(1, 4):
            copy = pltpu.make_async_remote_copy(
                src_ref=part.at[b],
                dst_ref=gathered.at[b, step - 1],
                send_sem=sum_send.at[b, step - 1],
                recv_sem=sum_recv.at[b, step - 1],
                device_id={"mp": (mine + step) % 4},
                device_id_type=MESH,
            )
            copy.start()
            copies.append(copy)
        return copies

    def back_copy(i, head):
        to = behind(OFFSETS[i])
        columns = pl.ds(head * chunk, chunk)
        return pltpu.make_async_remote_copy(
            src_ref=delta.at[rows_of(i), columns],
            dst_ref=back.at[rows_of(me), columns],
            send_sem=back_send.at[head, i],
            recv_sem=back_recv.at[head, i],
            device_id={"dp": to},
            device_id_type=MESH,
        )

    back_copies = {}

    def raise_up(b, copies):
        for copy in copies:
            copy.wait_recv()
        if b == 0:
            loads[3].wait()
            loads[4].wait()
        summed = (part[b] + gathered[b, 0]) + (gathered[b, 1] + gathered[b, 2])
        summed = summed.astype(jnp.bfloat16).astype(jnp.float32)
        first, second = summed[:block], summed[block:]
        first_turned = pltpu.roll(first, rank, 1)
        second_turned = pltpu.roll(second, rank, 1)
        half_left = left[:half_block]
        parts = [
            jnp.where(left, first, first_turned),
            jnp.where(left, first_turned, first),
            jnp.concatenate(
                [
                    jnp.where(half_left, second, second_turned),
                    jnp.where(half_left, second_turned, second),
                ],
                axis=0,
            ),
        ]
        want = wanted(b)
        spread = [
            jnp.concatenate(
                [
                    jnp.where(want == float(2 * p), one, 0.0).astype(jnp.bfloat16)
                    for p in range(adapters // 2)
                ],
                axis=1,
            )
            for one in parts
        ]
        here = pl.ds(b * block, block)
        depth = adapters * rank
        for head in range(kv_heads):
            start = head * per_head * D
            for c in range(0, per_head * D, 512):
                got = jnp.dot(
                    spread[0],
                    query_up[:, :, start + c : start + c + 512].reshape(depth, 512),
                    preferred_element_type=jnp.float32,
                )
                delta[here, head * chunk + c : head * chunk + c + 512] = (
                    adapter_scale * got
                ).astype(jnp.bfloat16)
        for j in range(2):
            got = jnp.dot(
                spread[1 + j],
                kv_up[:, j].reshape(depth, kv_heads * D),
                preferred_element_type=jnp.float32,
            )
            got = (adapter_scale * got).astype(jnp.bfloat16)
            for head in range(kv_heads):
                at = head * chunk + (per_head + j) * D
                delta[here, at : at + D] = got[:, head * D : (head + 1) * D]
        for head, which in SENDS[b]:
            for i in range(which * group_devices, (which + 1) * group_devices):
                if i == 0:
                    continue
                back_copies[head, i] = back_copy(i, head)
                back_copies[head, i].start()
        if b == 0:
            back[rows_of(me)] = delta[rows_of(0)]

    pending = None
    for b in range(blocks):
        started = project(b)
        if pending is not None:
            raise_up(b - 1, pending)
        pending = started
        if b == 0:
            sums = []
        sums.append(started)
    raise_up(blocks - 1, pending)

    for k in (5, 6, 10, 11):
        loads[k].wait()
    for k in range(2):
        base_new[:, k * kv_heads * D : (k + 1) * kv_heads * D] = base_kv[:, k, :].astype(
            jnp.float32
        )
    for i in range(1, len(OFFSETS)):
        page_copies[i].wait_recv()
    ext[pages:] = landing[...]

    pick = jnp.where(iota((rows, slots), 1) == target_col, 1.0, 0.0).astype(jnp.bfloat16)
    tokens = page_count * PAGE_TOKENS
    heads = kv_heads * per_head
    token = iota((heads, tokens), 1)
    upper = iota((heads, D), 0) < per_head
    scale = D**-0.5

    def store(head):
        columns = pl.ds(head * per_head * D, per_head * D)
        return pltpu.make_async_copy(
            out_ref.at[:, columns], out_hbm.at[:, columns], load_sem.at[12 + head]
        )

    for head in range(kv_heads):
        for i in range(1, len(OFFSETS)):
            back_copies[head, i].wait_recv()
        for g in range(0, per_head + 2, 2):
            got = jnp.dot(
                pick,
                back[:, head * chunk + g * D : head * chunk + (g + 2) * D],
                preferred_element_type=jnp.float32,
            )
            for k in range(2):
                one = got[:, k * D : (k + 1) * D]
                if g < per_head:
                    at = (head * per_head + g + k) * D
                    base = base_query[:, at : at + D]
                else:
                    at = (k * kv_heads + head) * D
                    base = base_new[:, at : at + D]
                value = (base.astype(jnp.float32) + one).astype(jnp.bfloat16).astype(jnp.float32)
                if g < per_head:
                    wide[:, head * per_head + g + k, :] = value
                else:
                    fresh[:, at : at + D] = value

    def gather(r, which):
        return jnp.concatenate([ext[table[p, r], which] for p in range(page_count)], axis=0)

    def per_row(r, at):
        new = fresh[pl.ds(r, 1), at : at + 2 * D]
        return jnp.concatenate(
            [
                jnp.broadcast_to(new[:, :D], (per_head, D)),
                jnp.broadcast_to(new[:, D:], (per_head, D)),
            ],
            axis=0,
        )

    def score(r):
        q = wide[r]
        zero = jnp.zeros_like(q)
        both = jnp.concatenate(
            [jnp.where(upper, q, zero), jnp.where(upper, zero, q)], axis=1
        ).astype(jnp.bfloat16)
        return lax.dot_general(
            both, gather(r, 0), (((1,), (1,)), ((), ())), preferred_element_type=jnp.float32
        )

    def soft(r, s):
        s = jnp.where(token < lens[0, r], s * scale, -jnp.inf)
        own = jnp.sum(wide[r] * per_row(r, 0), axis=1, keepdims=True) * scale
        top = jnp.maximum(jnp.max(s, axis=1, keepdims=True), own)
        p = jnp.exp(s - top)
        po = jnp.exp(own - top)
        inv = 1.0 / (jnp.sum(p, axis=1, keepdims=True) + po)
        own_weight = (po * inv).astype(jnp.bfloat16).astype(jnp.float32)
        return (p * inv).astype(jnp.bfloat16), own_weight * per_row(r, 2 * D)

    def weigh(r, p, own_part):
        o = jnp.dot(p, gather(r, 1), preferred_element_type=jnp.float32)
        wide[r] = jnp.where(upper, o[:, :D], o[:, D:]) + own_part

    def body(i, carry):
        at = i * GROUP
        scores = [score(at + j) for j in range(GROUP)]
        weights = [soft(at + j, scores[j]) for j in range(GROUP)]
        for j in range(GROUP):
            weigh(at + j, *weights[j])
        return carry

    lax.fori_loop(0, rows // GROUP, body, 0)
    for head in range(kv_heads):
        for g in range(per_head):
            at = (head * per_head + g) * D
            out_ref[:, at : at + D] = wide[:, head * per_head + g, :].astype(jnp.bfloat16)
        store(head).start()

    for i in range(1, len(OFFSETS)):
        row_copies[i].wait_send()
        page_copies[i].wait_send()
        for head in range(kv_heads):
            back_copies[head, i].wait_send()
    for copies in sums:
        for copy in copies:
            copy.wait_send()
    for head in range(kv_heads):
        store(head).wait()


def shards(
    hidden,
    base_query_rows,
    key_value_base,
    key_value_pool,
    request_page_table,
    context_length,
    handover_pages,
    request_adapter,
    adapter_position,
    adapter_down_weight,
    query_up_weight,
    key_value_up,
):
    rows, width = hidden.shape
    owners = handover_pages.shape[0]
    slots = owners * CAPACITY
    query_part = base_query_rows.shape[1]
    kv_part = key_value_base.shape[2]
    kv_heads = kv_part // HEAD_SIZE
    per_head = query_part // kv_part
    total = adapter_position.shape[0]
    rank = adapter_down_weight.shape[2]
    blocks = 4
    block = slots // blocks
    packed = block * 3 // 2
    pages = key_value_pool.shape[0]
    bf16, f32 = jnp.bfloat16, jnp.float32
    hbm = pl.BlockSpec(memory_space=pl.ANY)
    dma = pltpu.SemaphoreType.DMA
    return pl.pallas_call(
        fused,
        out_shape=jax.ShapeDtypeStruct((rows, query_part), bf16),
        in_specs=[hbm] * 12,
        out_specs=hbm,
        scratch_shapes=[
            pltpu.VMEM((1, rows), jnp.int32),
            pltpu.VMEM((1, total), jnp.int32),
            pltpu.SMEM(request_page_table.shape[::-1], jnp.int32),
            pltpu.SMEM((1, rows), jnp.int32),
            pltpu.SMEM(handover_pages.shape[::-1], jnp.int32),
            pltpu.VMEM((rows, query_part), bf16),
            pltpu.VMEM((rows, width), bf16),
            pltpu.VMEM((rows, query_part), bf16),
            pltpu.VMEM(key_value_base.shape, bf16),
            pltpu.VMEM((rows, 2 * kv_part), f32),
            pltpu.VMEM(adapter_down_weight.shape, bf16),
            pltpu.VMEM(query_up_weight.shape, bf16),
            pltpu.VMEM(key_value_up.shape, bf16),
            pltpu.VMEM((slots, width + HEAD_SIZE), bf16),
            pltpu.VMEM((slots, width + HEAD_SIZE), bf16),
            pltpu.VMEM((owners * MCAP,) + key_value_pool.shape[1:], bf16),
            pltpu.VMEM((owners * MCAP,) + key_value_pool.shape[1:], bf16),
            pltpu.VMEM((pages + owners * MCAP,) + key_value_pool.shape[1:], bf16),
            pltpu.VMEM((3, block, HEAD_SIZE), f32),
            pltpu.VMEM((blocks, packed, HEAD_SIZE), f32),
            pltpu.VMEM((blocks, 3, packed, HEAD_SIZE), f32),
            pltpu.VMEM((slots, query_part + 2 * kv_part), bf16),
            pltpu.VMEM((slots, query_part + 2 * kv_part), bf16),
            pltpu.VMEM((rows, kv_heads * per_head, HEAD_SIZE), f32),
            pltpu.VMEM((rows, 2 * kv_part), f32),
            dma((12 + kv_heads,)),
            dma((owners,)),
            dma((owners,)),
            dma((owners,)),
            dma((owners,)),
            dma((blocks, 3)),
            dma((blocks, 3)),
            dma((kv_heads, owners)),
            dma((kv_heads, owners)),
        ],
        compiler_params=pltpu.CompilerParams(
            collective_id=0, has_side_effects=True, vmem_limit_bytes=56 * 1024 * 1024
        ),
    )(
        request_adapter.reshape(1, rows),
        adapter_position.reshape(1, total),
        request_page_table.T,
        context_length.reshape(1, rows),
        handover_pages.T,
        hidden,
        base_query_rows,
        key_value_base,
        key_value_pool,
        adapter_down_weight,
        query_up_weight,
        key_value_up,
    )


def solution(mesh):
    return jax.shard_map(
        shards,
        mesh=mesh,
        in_specs=(
            P("dp", "mp"),
            P("dp", "mp"),
            P("dp", None, "mp"),
            P("dp", None, None, "mp"),
            P("dp", None),
            P("dp"),
            P("dp", None),
            P("dp"),
            P(),
            P("dp", None, None, "mp"),
            P("dp", None, "mp"),
            P("dp", None, None, "mp"),
        ),
        out_specs=P("dp", "mp"),
        check_vma=False,
    )
```
